512 devices in a mesh: row: 32 (over z, x_lo, core), col: 16 (over x_hi, y).
Axes of the slice: x: 4 (x_hi: 2, x_lo: 2; x = x_hi * 2 + x_lo), y: 8, z: 8, core: 2. Of those that a mesh axis runs over, the one named last changes fastest.
Arguments:
- object_field: float32 [3, 2, 4096, 2048], P(None, None, 'row', 'col'), may hold values from -5 to 5
- probe: float32 [2, 128, 128], replicated, may hold values from -5 to 5
- measured: float32 [32, 16, 2, 128, 128], P('row', 'col'), may hold values from 0.25 to 4
- positions: int32 [32, 16, 2, 2], P('row', 'col'), may hold values from 0 to 127
- counts: int32 [32, 16], P('row', 'col'), may hold values from 1 to 2, as said below
Outputs:
- object_next: float32 [3, 2, 4096, 2048], P(None, None, 'row', 'col')
The draws below stay inside these ranges and needn't reach their ends.
Inputs may be any that keep to these rules, and one draw needn't show every extreme that they name: Slots 0 to counts - 1 of a tile are live; some tile has all 2 live.
All inputs are finite; a program needn't handle non-finite values.
Results may differ from the reference program's by a relative error of at most 0.0003.
Values sent between devices are 32-bit elements; how exact they have to be, the bound alone decides.
No kernel may reach another device: no remote copies, remote signals or barrier semaphores. Data moves between devices by JAX's collectives and lax.ppermute only.
A program may use at most 64 MiB of HBM per device.

```python
import math
import jax
import jax.numpy as jnp
from jax import lax

W = 128
S = 128
SLICES = 3
ITERS = 2
SLOTS = 2
TILE_ROWS = 32
TILE_COLS = 16
ROWS_ALL = 4096
COLS_ALL = 2048


def draw_counts(key, part):
    first_key = jax.random.fold_in(key, 11)
    second_key = jax.random.fold_in(key, 12)
    third_key = jax.random.fold_in(key, 13)
    first_draw = jax.random.randint(first_key, (TILE_ROWS, TILE_COLS), 1, SLOTS + 1, dtype=jnp.int32)
    second_draw = jax.random.randint(second_key, (TILE_ROWS, TILE_COLS), 1, SLOTS + 1, dtype=jnp.int32)
    busiest = jax.random.randint(third_key, (), 0, TILE_ROWS * TILE_COLS, dtype=jnp.int32)
    ordinal = jnp.arange(TILE_ROWS * TILE_COLS, dtype=jnp.int32).reshape(TILE_ROWS, TILE_COLS)
    return jnp.where(ordinal == busiest, SLOTS, jnp.minimum(first_draw, second_draw)).astype(jnp.int32)


def place_ends(entries, key, least, high):
    longest = entries.shape.index(max(entries.shape))
    spots = []
    for shift in (0, 1):
        where = [jax.random.randint(jax.random.fold_in(key, axis), (), 0, length) for axis, length in enumerate(entries.shape)]
        where[longest] = (where[longest] + shift) % entries.shape[longest]
        spots.append(tuple(where))
    return entries.at[spots[0]].set(least).at[spots[1]].set(high)


def steps_of(rng, extent, split, low, largest):
    def one(dim, parts):
        steps = jax.random.uniform(jax.random.fold_in(jax.random.fold_in(rng, 6), dim), (parts,), jnp.float32, low / len(split), largest / len(split))
        return jnp.repeat(jnp.exp(steps), extent[dim] // parts).reshape((-1,) + (1,) * (len(extent) - dim - 1))

    factor_of = one(*split[0])
    for cut in split[1:]:
        factor_of = factor_of * one(*cut)
    return factor_of


def centred(stream_key, shape, scale, reach, shards=(), kind=jnp.bfloat16):
    drawn = scale * jax.random.normal(stream_key, shape, jnp.float32)
    if shards:
        drawn = drawn * steps_of(stream_key, shape, shards, -0.22, 0.18)
    return jnp.clip(drawn, -reach, reach).astype(kind)


def setup_inputs(seed: int = 0) -> dict:
    streams_of = jax.random.split(jax.random.key(seed), 6)
    return {
        "object_field": centred(streams_of[0], (SLICES, 2, ROWS_ALL, COLS_ALL), 0.7, 5.0, ((2, 32), (3, 16)), jnp.float32),
        "probe": centred(streams_of[1], (2, W, W), 0.7, 5.0, (), jnp.float32),
        "measured": jnp.clip(jnp.exp(math.log(4.0) - 2.7725887 * jax.random.uniform(streams_of[2], (TILE_ROWS, TILE_COLS, SLOTS, W, W), jnp.float32) ** steps_of(streams_of[2], (TILE_ROWS, TILE_COLS, SLOTS, W, W), ((0, 32), (1, 16)), -0.2, 0.2)), 0.25, 4.0),
        "positions": place_ends(jax.random.randint(streams_of[3], (TILE_ROWS, TILE_COLS, SLOTS, 2), 0, S), jax.random.fold_in(streams_of[3], 1), 0, S - 1).astype(jnp.int32),
        "counts": draw_counts(jax.random.fold_in(streams_of[5], 71), 0),
    }


LEARNING_RATE = 0.02


def phase_table():
    frequency = (jnp.arange(W, dtype=jnp.int32) + W // 2) % W - W // 2
    squares = (frequency[:, None] * frequency[:, None] + frequency[None, :] * frequency[None, :]).astype(jnp.float32)
    angles = (-0.25 * math.pi / W) * squares
    return lax.complex(jnp.cos(angles), jnp.sin(angles))


def propagate(wavefield, kernel):
    return jnp.fft.ifft2(jnp.fft.fft2(wavefield, norm="ortho") * kernel, norm="ortho")


def window_gradient(window, probe_wave, sample, kernel):
    layers = [lax.complex(window[slice_index, 0], window[slice_index, 1]) for slice_index in range(SLICES)]
    wavefield = probe_wave
    incident = []
    for slice_index in range(SLICES):
        incident.append(wavefield)
        wavefield = layers[slice_index] * wavefield
        if slice_index + 1 < SLICES:
            wavefield = propagate(wavefield, kernel)
    far_field = jnp.fft.fft2(wavefield, norm="ortho")
    residue = jnp.real(far_field) ** 2 + jnp.imag(far_field) ** 2 - sample
    back_wave = jnp.fft.ifft2(residue * far_field, norm="ortho")
    pieces = [None] * SLICES
    for slice_index in reversed(range(SLICES)):
        product = jnp.conj(incident[slice_index]) * back_wave
        pieces[slice_index] = jnp.stack([jnp.real(product), jnp.imag(product)])
        if slice_index > 0:
            back_wave = propagate(jnp.conj(layers[slice_index]) * back_wave, jnp.conj(kernel))
    return jnp.stack(pieces)


def reference(object_field, probe, measured, positions, counts):
    rim_width = W // 2
    kernel = phase_table()
    probe_wave = lax.complex(probe[0], probe[1])
    total_windows = TILE_ROWS * TILE_COLS * SLOTS
    flat_corners = positions.reshape(total_windows, 2).astype(jnp.int32)
    flat_samples = measured.reshape(total_windows, W, W)
    ordinal = jnp.arange(total_windows, dtype=jnp.int32)
    tile_number = ordinal // SLOTS
    live_mask = (ordinal % SLOTS < counts.reshape(-1).astype(jnp.int32)[tile_number]).astype(object_field.dtype)
    row_start = ((tile_number // TILE_COLS) * S + flat_corners[:, 0]).astype(jnp.int32)
    col_start = ((tile_number % TILE_COLS) * S + flat_corners[:, 1]).astype(jnp.int32)
    anchor = jnp.zeros((), jnp.int32)
    current = object_field
    for iteration in range(ITERS):
        padded = jnp.pad(current, ((0, 0), (0, 0), (rim_width, rim_width), (rim_width, rim_width)))

        def visit(window_index, running):
            corner_start = (anchor, anchor, row_start[window_index], col_start[window_index])
            window = lax.dynamic_slice(padded, corner_start, (SLICES, 2, W, W))
            update = window_gradient(window, probe_wave, flat_samples[window_index], kernel) * live_mask[window_index]
            before = lax.dynamic_slice(running, corner_start, (SLICES, 2, W, W))
            return lax.dynamic_update_slice(running, before + update.astype(running.dtype), corner_start)

        gradient_sum = lax.fori_loop(0, total_windows, visit, jnp.zeros_like(padded))
        interior = gradient_sum[:, :, rim_width:rim_width + TILE_ROWS * S, rim_width:rim_width + TILE_COLS * S]
        current = current - LEARNING_RATE * interior
    return current
```

```python
import functools
import math

import jax
import jax.numpy as jnp
import ml_dtypes
import numpy as np
from jax import lax
from jax.experimental import pallas as pl
from jax.experimental.pallas import tpu as pltpu
from jax.sharding import PartitionSpec as P

ITERS = 2
LEARNING_RATE = 0.02
F32 = jnp.float32
BF16 = jnp.bfloat16
VMEM = pl.BlockSpec(memory_space=pltpu.VMEM)
SMEM = pl.BlockSpec(memory_space=pltpu.SMEM)
PARAMS = pltpu.CompilerParams(vmem_limit_bytes=48 * 1024 * 1024)


def make_tables(side):
    ordinal = np.arange(side, dtype=np.int64)
    angles = -2.0 * math.pi / side * (ordinal[:, None] * ordinal[None, :] % side)
    cosine, sine = np.cos(angles) / math.sqrt(side), np.sin(angles) / math.sqrt(side)
    forward = np.block([[cosine, sine], [-sine, cosine]])
    tables = []
    for matrix in (forward, forward.T):
        high = matrix.astype(np.float32).astype(ml_dtypes.bfloat16)
        low = (matrix - high.astype(np.float64)).astype(np.float32).astype(ml_dtypes.bfloat16)
        tables += [high, low]
    frequency = (ordinal + side // 2) % side - side // 2
    phases = -0.25 * math.pi / side * (frequency[:, None] ** 2 + frequency[None, :] ** 2)
    kernel = np.stack([np.cos(phases), np.sin(phases)]).astype(np.float32)
    return tables + [kernel]


def split(values):
    high = values.astype(BF16)
    return high, (values - high.astype(F32)).astype(BF16)


def dot(left, right):
    return jnp.dot(left, right, preferred_element_type=F32)


def right_mul(field, high, low):
    real, imag = field
    side = real[0].shape[0]
    stacked = jnp.concatenate(
        [jnp.concatenate([r, i], axis=1) for r, i in zip(real, imag)], axis=0
    )
    x_high, x_low = split(stacked)
    out = dot(x_high, high[...]) + (dot(x_high, low[...]) + dot(x_low, high[...]))
    rows = [out[j * side : (j + 1) * side] for j in range(len(real))]
    return [r[:, :side] for r in rows], [r[:, side:] for r in rows]


def left_mul(field, high, low):
    real, imag = field
    side = real[0].shape[0]
    stacked = jnp.concatenate(
        [jnp.concatenate(real, axis=1), jnp.concatenate(imag, axis=1)], axis=0
    )
    x_high, x_low = split(stacked)
    out = dot(high[...], x_high) + (dot(low[...], x_high) + dot(high[...], x_low))
    cols = [out[:, j * side : (j + 1) * side] for j in range(len(real))]
    return [c[:side] for c in cols], [c[side:] for c in cols]


def times(a, b):
    return (
        [x * u - y * v for x, y, u, v in zip(a[0], a[1], b[0], b[1])],
        [x * v + y * u for x, y, u, v in zip(a[0], a[1], b[0], b[1])],
    )


def conj_times(a, b):
    return (
        [x * u + y * v for x, y, u, v in zip(a[0], a[1], b[0], b[1])],
        [x * v - y * u for x, y, u, v in zip(a[0], a[1], b[0], b[1])],
    )


def lanes(shape):
    return lax.broadcasted_iota(jnp.int32, shape, len(shape) - 1)


def pack_body(tile, to_right, to_left):
    layers, _, side, _ = tile.shape
    low = lanes((side, side)) < side // 2
    for s in range(layers):
        real, turned = tile[s, 0], pltpu.roll(tile[s, 1], side // 2, 1)
        to_right[s] = jnp.where(low, turned, real)
        to_left[s] = jnp.where(low, real, turned)


def unpacked(from_left, from_right, low, half):
    real = jnp.where(low, from_right, from_left)
    imag = pltpu.roll(jnp.where(low, from_left, from_right), half, 1)
    return real, imag


def rows_out(blocks, s, c, to_below, to_above, half):
    for k, block in enumerate(blocks):
        to_above[k, s, c] = block[:half]
        to_below[k, s, c] = block[half:]


def halo_body(tile, from_left, from_right, side_block, to_below, to_above):
    layers, _, side, _ = tile.shape
    half = side // 2
    low = lanes((side, side)) < half
    for s in range(layers):
        parts = unpacked(from_left[s], from_right[s], low, half)
        for c in range(2):
            side_block[s, c] = parts[c]
            rows_out((tile[s, c], parts[c]), s, c, to_below, to_above, half)


def slots_body(
    corners, counts, tile, side_block, from_above, from_below, probe, measured,
    fwd_high, fwd_low, inv_high, inv_low, phase,
    grad_tile, grad_side, to_below, to_above, turning, windows, incident,
):
    layers, _, side, _ = tile.shape
    half = side // 2
    slots = corners.shape[0]
    row = lax.broadcasted_iota(jnp.int32, (side, side), 0)
    lane = lax.broadcasted_iota(jnp.int32, (side, side), 1)
    row_in, lane_in, row_back, row_fwd, lane_back, lane_fwd = [], [], [], [], [], []
    for j in range(slots):
        p, q = corners[j, 0] - half, corners[j, 1] - half
        row_in.append((row >= p) & (row < p + side))
        lane_in.append((lane >= q) & (lane < q + side))
        row_back.append(lax.rem(p + side, side))
        row_fwd.append(lax.rem(side - p, side))
        lane_back.append(lax.rem(side - q, side))
        lane_fwd.append(lax.rem(q + side, side))
    for s in range(layers):
        for c in range(2):
            row_block = jnp.concatenate([from_below[0, s, c], from_above[0, s, c]], axis=0)
            both_block = jnp.concatenate([from_below[1, s, c], from_above[1, s, c]], axis=0)
            for j in range(slots):
                inner = jnp.where(lane_in[j], tile[s, c], side_block[s, c])
                outer = jnp.where(lane_in[j], row_block, both_block)
                mixed = pltpu.roll(jnp.where(row_in[j], inner, outer), lane_back[j], 1)
                place = turning.at[(s * 2 + c) * slots + j]
                place[:side] = mixed
                place[side:] = mixed
                windows[s, c, j] = place[pl.ds(row_back[j], side), :]

    def layer(s):
        return [windows[s, 0, j] for j in range(slots)], [windows[s, 1, j] for j in range(slots)]

    def incoming(s):
        if s == 0:
            return [probe[0]] * slots, [probe[1]] * slots
        return [incident[s - 1, 0, j] for j in range(slots)], [
            incident[s - 1, 1, j] for j in range(slots)
        ]

    def propagate(field, weight):
        field = left_mul(right_mul(field, fwd_high, fwd_low), inv_high, inv_low)
        field = weight(([phase[0]] * slots, [phase[1]] * slots), field)
        return right_mul(left_mul(field, fwd_high, fwd_low), inv_high, inv_low)

    for s in range(layers):
        wave = times(layer(s), incoming(s))
        if s + 1 < layers:
            wave = propagate(wave, times)
            for c in range(2):
                for j in range(slots):
                    incident[s, c, j] = wave[c][j]
    far = left_mul(right_mul(wave, fwd_high, fwd_low), inv_high, inv_low)
    residue = [
        far[0][j] * far[0][j] + far[1][j] * far[1][j] - measured[0, 0, j] for j in range(slots)
    ]
    back = ([a * b for a, b in zip(residue, far[0])], [a * b for a, b in zip(residue, far[1])])
    back = right_mul(left_mul(back, fwd_high, fwd_low), inv_high, inv_low)
    for s in reversed(range(layers)):
        product = conj_times(incoming(s), back)
        for c in range(2):
            moved = []
            for j in range(slots):
                turned = pltpu.roll(product[c][j], lane_fwd[j], 1)
                place = turning.at[(s * 2 + c) * slots + j]
                place[:side] = turned
                place[side:] = turned
                live = j < counts[0]
                moved.append(jnp.where(live, place[pl.ds(row_fwd[j], side), :], 0.0))

            def total(rows_of, lanes_of):
                terms = [
                    jnp.where(rows_of(row_in[j]) & lanes_of(lane_in[j]), moved[j], 0.0)
                    for j in range(slots)
                ]
                return functools.reduce(lambda a, b: a + b, terms)

            same, other = (lambda m: m), (lambda m: ~m)
            grad_tile[s, c] = total(same, same)
            grad_side[s, c] = total(same, other)
            for k, lanes_of in enumerate((same, other)):
                block = total(other, lanes_of)
                to_below[k, s, c] = block[:half]
                to_above[k, s, c] = block[half:]
        if s > 0:
            back = propagate(conj_times(layer(s), back), conj_times)


def joined_rows(grad, k, from_above, from_below, s, c):
    return grad[s, c] + jnp.concatenate([from_above[k, s, c], from_below[k, s, c]], axis=0)


def middle_body(grad_tile, grad_side, from_above, from_below, new_tile, new_side, to_right, to_left):
    layers, _, side, _ = grad_tile.shape
    low = lanes((side, side)) < side // 2
    for s in range(layers):
        for c in range(2):
            inner = joined_rows(grad_tile, 0, from_above, from_below, s, c)
            outer = joined_rows(grad_side, 1, from_above, from_below, s, c)
            new_tile[s, c] = inner
            new_side[s, c] = outer
            to_right[s, c] = jnp.where(low, outer, inner)
            to_left[s, c] = jnp.where(low, inner, outer)


def step_body(
    tile, side_block, grad_tile, grad_side, from_left, from_right, new_tile, new_side, to_below, to_above
):
    layers, _, side, _ = tile.shape
    half = side // 2
    col, cols = lax.axis_index("col"), lax.axis_size("col")
    lane = lanes((side, side))
    low = lane < half
    first = jnp.where(col + 1 < cols, 0, half)
    last = jnp.where(col > 0, side, half)
    on_grid = (lane >= first) & (lane < last)
    for s in range(layers):
        for c in range(2):
            left, right = from_left[s, c], from_right[s, c]
            inner = grad_tile[s, c] + jnp.where(low, left, right)
            outer = grad_side[s, c] + jnp.where(low, right, left)
            inner = tile[s, c] - LEARNING_RATE * inner
            outer = jnp.where(on_grid, side_block[s, c] - LEARNING_RATE * outer, 0.0)
            new_tile[s, c] = inner
            new_side[s, c] = outer
            rows_out((inner, outer), s, c, to_below, to_above, half)


def last_rows_body(grad_tile, grad_side, from_above, from_below, new_tile, to_right, to_left):
    layers, _, side, _ = grad_tile.shape
    half = side // 2
    low = lanes((side, side)) < half
    for s in range(layers):
        outer = []
        for c in range(2):
            new_tile[s, c] = joined_rows(grad_tile, 0, from_above, from_below, s, c)
            outer.append(joined_rows(grad_side, 1, from_above, from_below, s, c))
        turned = pltpu.roll(outer[1], half, 1)
        to_right[s] = jnp.where(low, outer[0], turned)
        to_left[s] = jnp.where(low, turned, outer[0])


def last_body(tile, grad_tile, from_left, from_right, out):
    layers, _, side, _ = tile.shape
    half = side // 2
    low = lanes((side, side)) < half
    for s in range(layers):
        real = jnp.where(low, from_left[s], from_right[s])
        imag = pltpu.roll(jnp.where(low, from_right[s], from_left[s]), half, 1)
        for c, part in enumerate((real, imag)):
            out[s, c] = tile[s, c] - LEARNING_RATE * (grad_tile[s, c] + part)


def call(body, shapes, *operands, specs=None, scratch=(), name=None, flops=0):
    return pl.pallas_call(
        body,
        out_shape=[jax.ShapeDtypeStruct(shape, F32) for shape in shapes],
        in_specs=specs or [VMEM] * len(operands),
        out_specs=[VMEM] * len(shapes),
        scratch_shapes=list(scratch),
        compiler_params=PARAMS,
        name=name,
        cost_estimate=pl.CostEstimate(
            flops=flops,
            bytes_accessed=sum(4 * math.prod(shape) for shape in shapes),
            transcendentals=0,
        ),
    )(*operands)


def both_ways(axis, up, down):
    count = lax.axis_size(axis)
    forward = [(i, i + 1) for i in range(count - 1)]
    backward = [(target, source) for source, target in forward]
    return lax.ppermute(up, axis, forward), lax.ppermute(down, axis, backward)


def shards(object_field, probe, measured, positions, counts):
    layers, _, side, _ = object_field.shape
    half = side // 2
    slots = positions.shape[2]
    corners = positions.reshape(slots, 2)
    live = counts.reshape(1)
    tables = [jnp.asarray(table) for table in make_tables(side)]
    whole, packed, strips = (layers, 2, side, side), (layers, side, side), (2, layers, 2, half, side)
    scratch = (
        pltpu.VMEM((layers * 2 * slots, 2 * side, side), F32),
        pltpu.VMEM((layers, 2, slots, side, side), F32),
        pltpu.VMEM((layers - 1, 2, slots, side, side), F32),
    )
    products = 4 * layers - 2
    flops = products * 2 * 3 * 2 * (2 * side) ** 2 * (slots * side)
    tile = object_field
    sent = call(pack_body, (packed, packed), tile, name="pack")
    from_left, from_right = both_ways("col", *sent)
    side_block, *sent = call(
        halo_body, (whole, strips, strips), tile, from_left, from_right, name="halo"
    )
    for iteration in range(ITERS):
        from_above, from_below = both_ways("row", *sent)
        grad_tile, grad_side, *sent = call(
            slots_body,
            (whole, whole, strips, strips),
            corners, live, tile, side_block, from_above, from_below, probe, measured, *tables,
            specs=[SMEM, SMEM] + [VMEM] * (6 + len(tables)),
            scratch=scratch,
            name="slots",
            flops=flops,
        )
        from_above, from_below = both_ways("row", *sent)
        if iteration + 1 < ITERS:
            grad_tile, grad_side, *sent = call(
                middle_body, (whole, whole, whole, whole), grad_tile, grad_side, from_above, from_below, name="middle"
            )
            from_left, from_right = both_ways("col", *sent)
            tile, side_block, *sent = call(
                step_body,
                (whole, whole, strips, strips),
                tile, side_block, grad_tile, grad_side, from_left, from_right,
                name="step",
            )
        else:
            grad_tile, *sent = call(
                last_rows_body, (whole, packed, packed), grad_tile, grad_side, from_above, from_below, name="last_rows"
            )
            from_left, from_right = both_ways("col", *sent)
            (tile,) = call(last_body, (whole,), tile, grad_tile, from_left, from_right, name="last")
    return tile


def solution(mesh):
    placed = (
        P(None, None, "row", "col"),
        P(),
        P("row", "col", None, None, None),
        P("row", "col", None, None),
        P("row", "col"),
    )
    return jax.shard_map(
        shards, mesh=mesh, in_specs=placed, out_specs=P(None, None, "row", "col"), check_vma=False
    )
```

```python
import functools
import math

import jax
import jax.numpy as jnp
import ml_dtypes
import numpy as np
from jax import lax
from jax.experimental import pallas as pl
from jax.experimental.pallas import tpu as pltpu
from jax.sharding import PartitionSpec as P

ITERS = 2
LEARNING_RATE = 0.02
F32 = jnp.float32
BF16 = jnp.bfloat16
VMEM = pl.BlockSpec(memory_space=pltpu.VMEM)
SMEM = pl.BlockSpec(memory_space=pltpu.SMEM)
PARAMS = pltpu.CompilerParams(vmem_limit_bytes=48 * 1024 * 1024)


def make_tables(side):
    ordinal = np.arange(side, dtype=np.int64)
    angles = -2.0 * math.pi / side * (ordinal[:, None] * ordinal[None, :] % side)
    transform = np.exp(1j * angles) / math.sqrt(side)
    frequency = (ordinal + side // 2) % side - side // 2
    phases = np.exp(-0.25j * math.pi / side * frequency**2)
    spread = transform.conj() @ (phases[:, None] * transform)
    tables = []
    for matrix in (transform, spread):
        block = np.block([[matrix.real, matrix.imag], [-matrix.imag, matrix.real]])
        for part in (block, block.T):
            high = part.astype(np.float32).astype(ml_dtypes.bfloat16)
            low = (part - high.astype(np.float64)).astype(np.float32).astype(ml_dtypes.bfloat16)
            tables += [high, low]
    return tables


def split(values):
    high = values.astype(BF16)
    return high, (values - high.astype(F32)).astype(BF16)


def dot(left, right):
    return jnp.dot(left, right, preferred_element_type=F32)


def right_mul(field, table):
    high, low = table
    deep = jnp.concatenate([high[...], high[...], low[...]], axis=0)
    reals, imags = [], []
    for real, imag in zip(*field):
        side = real.shape[0]
        x_high, x_low = split(jnp.concatenate([real, imag], axis=1))
        out = dot(jnp.concatenate([x_high, x_low, x_high], axis=1), deep)
        reals.append(out[:, :side])
        imags.append(out[:, side:])
    return reals, imags


def left_mul(field, table):
    high, low = table
    reals, imags = [], []
    for real, imag in zip(*field):
        side = real.shape[0]
        x_high, x_low = split(jnp.concatenate([real, imag], axis=0))
        wide = dot(high[...], jnp.concatenate([x_high, x_low], axis=1))
        out = wide[:, :side] + wide[:, side:] + dot(low[...], x_high)
        reals.append(out[:side])
        imags.append(out[side:])
    return reals, imags


def both_mul(field, table, turned):
    return left_mul(right_mul(field, table), turned)


def times(a, b):
    return (
        [x * u - y * v for x, y, u, v in zip(a[0], a[1], b[0], b[1])],
        [x * v + y * u for x, y, u, v in zip(a[0], a[1], b[0], b[1])],
    )


def conj_times(a, b):
    return (
        [x * u + y * v for x, y, u, v in zip(a[0], a[1], b[0], b[1])],
        [x * v - y * u for x, y, u, v in zip(a[0], a[1], b[0], b[1])],
    )


def lanes(shape):
    return lax.broadcasted_iota(jnp.int32, shape, len(shape) - 1)


def halves(side, flipped):
    return (lanes((side, side)) < side // 2) != flipped


def odd_column():
    return lax.rem(lax.axis_index("col"), 2) == 1


def pack_body(tile, near, far):
    layers, _, side, _ = tile.shape
    pick = halves(side, odd_column())
    for s in range(layers):
        real, turned = tile[s, 0], pltpu.roll(tile[s, 1], side // 2, 1)
        near[s] = jnp.where(pick, real, turned)
        far[s] = jnp.where(pick, turned, real)


def rows_out(blocks, s, c, to_below, to_above, half):
    for k, block in enumerate(blocks):
        to_above[k, s, c] = block[:half]
        to_below[k, s, c] = block[half:]


def halo_body(tile, near, far, side_block, to_below, to_above):
    layers, _, side, _ = tile.shape
    half = side // 2
    pick = halves(side, odd_column())
    for s in range(layers):
        parts = jnp.where(pick, far[s], near[s]), pltpu.roll(jnp.where(pick, near[s], far[s]), half, 1)
        for c in range(2):
            side_block[s, c] = parts[c]
            rows_out((tile[s, c], parts[c]), s, c, to_below, to_above, half)


def slots_body(
    corners, counts, tile, side_block, from_above, from_below, probe, measured,
    fwd_high, fwd_low, inv_high, inv_low, on_high, on_low, off_high, off_low,
    grad_tile, grad_side, to_below, to_above, turning, windows, incident,
):
    layers, _, side, _ = tile.shape
    half = side // 2
    slots = corners.shape[0]
    row = lax.broadcasted_iota(jnp.int32, (side, side), 0)
    lane = lax.broadcasted_iota(jnp.int32, (side, side), 1)
    row_in, lane_in, row_back, row_fwd, lane_back, lane_fwd = [], [], [], [], [], []
    for j in range(slots):
        p, q = corners[j, 0] - half, corners[j, 1] - half
        row_in.append((row >= p) & (row < p + side))
        lane_in.append((lane >= q) & (lane < q + side))
        row_back.append(lax.rem(p + side, side))
        row_fwd.append(lax.rem(side - p, side))
        lane_back.append(lax.rem(side - q, side))
        lane_fwd.append(lax.rem(q + side, side))
    def cut(s):
        for c in range(2):
            row_block = jnp.concatenate([from_below[0, s, c], from_above[0, s, c]], axis=0)
            both_block = jnp.concatenate([from_below[1, s, c], from_above[1, s, c]], axis=0)
            for j in range(slots):
                inner = jnp.where(lane_in[j], tile[s, c], side_block[s, c])
                outer = jnp.where(lane_in[j], row_block, both_block)
                mixed = pltpu.roll(jnp.where(row_in[j], inner, outer), lane_back[j], 1)
                place = turning.at[(s * 2 + c) * slots + j]
                place[:side] = mixed
                place[side:] = mixed
                windows[s, c, j] = place[pl.ds(row_back[j], side), :]

    def layer(s):
        return [windows[s, 0, j] for j in range(slots)], [windows[s, 1, j] for j in range(slots)]

    def incoming(s):
        if s == 0:
            return [probe[0]] * slots, [probe[1]] * slots
        return [incident[s - 1, 0, j] for j in range(slots)], [
            incident[s - 1, 1, j] for j in range(slots)
        ]

    fwd, inv, on, off = (fwd_high, fwd_low), (inv_high, inv_low), (on_high, on_low), (off_high, off_low)
    cut(0)
    for s in range(layers):
        wave = times(layer(s), incoming(s))
        if s + 1 < layers:
            cut(s + 1)
            wave = both_mul(wave, on, off)
            for c in range(2):
                for j in range(slots):
                    incident[s, c, j] = wave[c][j]
    far = both_mul(wave, fwd, inv)
    residue = [
        far[0][j] * far[0][j] + far[1][j] * far[1][j] - measured[0, 0, j] for j in range(slots)
    ]
    back = ([a * b for a, b in zip(residue, far[0])], [a * b for a, b in zip(residue, far[1])])
    back = both_mul(back, inv, fwd)
    for s in reversed(range(layers)):
        product = conj_times(incoming(s), back)
        for c in range(2):
            moved = []
            for j in range(slots):
                turned = pltpu.roll(product[c][j], lane_fwd[j], 1)
                place = turning.at[(s * 2 + c) * slots + j]
                place[:side] = turned
                place[side:] = turned
                live = j < counts[0]
                moved.append(jnp.where(live, place[pl.ds(row_fwd[j], side), :], 0.0))

            def total(rows_of, lanes_of):
                terms = [
                    jnp.where(rows_of(row_in[j]) & lanes_of(lane_in[j]), moved[j], 0.0)
                    for j in range(slots)
                ]
                return functools.reduce(lambda a, b: a + b, terms)

            same, other = (lambda m: m), (lambda m: ~m)
            grad_tile[s, c] = total(same, same)
            grad_side[s, c] = total(same, other)
            for k, lanes_of in enumerate((same, other)):
                block = total(other, lanes_of)
                to_below[k, s, c] = block[:half]
                to_above[k, s, c] = block[half:]
        if s > 0:
            back = both_mul(conj_times(layer(s), back), off, on)


def joined_rows(grad, k, from_above, from_below, s, c):
    return grad[s, c] + jnp.concatenate([from_above[k, s, c], from_below[k, s, c]], axis=0)


def middle_body(grad_tile, grad_side, from_above, from_below, new_tile, new_side, near, far):
    layers, _, side, _ = grad_tile.shape
    pick = halves(side, odd_column())
    for s in range(layers):
        for c in range(2):
            inner = joined_rows(grad_tile, 0, from_above, from_below, s, c)
            outer = joined_rows(grad_side, 1, from_above, from_below, s, c)
            new_tile[s, c] = inner
            new_side[s, c] = outer
            near[s, c] = jnp.where(pick, inner, outer)
            far[s, c] = jnp.where(pick, outer, inner)


def step_body(
    tile, side_block, grad_tile, grad_side, near, far, new_tile, new_side, to_below, to_above
):
    layers, _, side, _ = tile.shape
    half = side // 2
    pick = halves(side, odd_column())
    col, cols = lax.axis_index("col"), lax.axis_size("col")
    lane = lanes((side, side))
    first = jnp.where(col + 1 < cols, 0, half)
    last = jnp.where(col > 0, side, half)
    on_grid = (lane >= first) & (lane < last)
    for s in range(layers):
        for c in range(2):
            inner = grad_tile[s, c] + jnp.where(pick, near[s, c], far[s, c])
            outer = grad_side[s, c] + jnp.where(pick, far[s, c], near[s, c])
            inner = tile[s, c] - LEARNING_RATE * inner
            outer = jnp.where(on_grid, side_block[s, c] - LEARNING_RATE * outer, 0.0)
            new_tile[s, c] = inner
            new_side[s, c] = outer
            rows_out((inner, outer), s, c, to_below, to_above, half)


def last_rows_body(grad_tile, grad_side, from_above, from_below, new_tile, near, far):
    layers, _, side, _ = grad_tile.shape
    half = side // 2
    pick = halves(side, odd_column())
    for s in range(layers):
        outer = []
        for c in range(2):
            new_tile[s, c] = joined_rows(grad_tile, 0, from_above, from_below, s, c)
            outer.append(joined_rows(grad_side, 1, from_above, from_below, s, c))
        turned = pltpu.roll(outer[1], half, 1)
        near[s] = jnp.where(pick, turned, outer[0])
        far[s] = jnp.where(pick, outer[0], turned)


def last_body(tile, grad_tile, near, far, out):
    layers, _, side, _ = tile.shape
    half = side // 2
    pick = halves(side, odd_column())
    for s in range(layers):
        real = jnp.where(pick, near[s], far[s])
        imag = pltpu.roll(jnp.where(pick, far[s], near[s]), half, 1)
        for c, part in enumerate((real, imag)):
            out[s, c] = tile[s, c] - LEARNING_RATE * (grad_tile[s, c] + part)


def call(body, shapes, *operands, specs=None, scratch=(), name=None, flops=0):
    return pl.pallas_call(
        body,
        out_shape=[jax.ShapeDtypeStruct(shape, F32) for shape in shapes],
        in_specs=specs or [VMEM] * len(operands),
        out_specs=[VMEM] * len(shapes),
        scratch_shapes=list(scratch),
        compiler_params=PARAMS,
        name=name,
        cost_estimate=pl.CostEstimate(
            flops=flops,
            bytes_accessed=sum(4 * math.prod(shape) for shape in shapes),
            transcendentals=0,
        ),
    )(*operands)


def along_rows(below, above):
    count = lax.axis_size("row")
    down = [(i, i + 1) for i in range(count - 1)]
    up = [(target, source) for source, target in down]
    return lax.ppermute(below, "row", down), lax.ppermute(above, "row", up)


def across_columns(near, far):
    count = lax.axis_size("col")
    trades = []
    for block, start in ((near, 1), (far, 0)):
        pairs = [(i, i + 1) for i in range(start, count - 1, 2)]
        trades.append(lax.ppermute(block, "col", pairs + [(j, i) for i, j in pairs]))
    return trades


def shards(object_field, probe, measured, positions, counts):
    layers, _, side, _ = object_field.shape
    half = side // 2
    slots = positions.shape[2]
    corners = positions.reshape(slots, 2)
    live = counts.reshape(1)
    tables = [jnp.asarray(table) for table in make_tables(side)]
    whole, packed, strips = (layers, 2, side, side), (layers, side, side), (2, layers, 2, half, side)
    scratch = (
        pltpu.VMEM((layers * 2 * slots, 2 * side, side), F32),
        pltpu.VMEM((layers, 2, slots, side, side), F32),
        pltpu.VMEM((layers - 1, 2, slots, side, side), F32),
    )
    products = 2 * layers
    flops = products * 2 * 3 * 2 * (2 * side) ** 2 * (slots * side)
    tile = object_field
    sent = call(pack_body, (packed, packed), tile, name="pack")
    side_block, *sent = call(
        halo_body, (whole, strips, strips), tile, *across_columns(*sent), name="halo"
    )
    for iteration in range(ITERS):
        from_above, from_below = along_rows(*sent)
        grad_tile, grad_side, *sent = call(
            slots_body,
            (whole, whole, strips, strips),
            corners, live, tile, side_block, from_above, from_below, probe, measured, *tables,
            specs=[SMEM, SMEM] + [VMEM] * (6 + len(tables)),
            scratch=scratch,
            name="slots",
            flops=flops,
        )
        from_above, from_below = along_rows(*sent)
        if iteration + 1 < ITERS:
            grad_tile, grad_side, *sent = call(
                middle_body, (whole, whole, whole, whole), grad_tile, grad_side, from_above, from_below, name="middle"
            )
            tile, side_block, *sent = call(
                step_body,
                (whole, whole, strips, strips),
                tile, side_block, grad_tile, grad_side, *across_columns(*sent),
                name="step",
            )
        else:
            grad_tile, *sent = call(
                last_rows_body, (whole, packed, packed), grad_tile, grad_side, from_above, from_below, name="last_rows"
            )
            (tile,) = call(last_body, (whole,), tile, grad_tile, *across_columns(*sent), name="last")
    return tile


def solution(mesh):
    placed = (
        P(None, None, "row", "col"),
        P(),
        P("row", "col", None, None, None),
        P("row", "col", None, None),
        P("row", "col"),
    )
    return jax.shard_map(
        shards, mesh=mesh, in_specs=placed, out_specs=P(None, None, "row", "col"), check_vma=False
    )
```

```python
import functools
import math

import jax
import jax.numpy as jnp
import ml_dtypes
import numpy as np
from jax import lax
from jax.experimental import pallas as pl
from jax.experimental.pallas import tpu as pltpu
from jax.sharding import PartitionSpec as P

ITERS = 2
LEARNING_RATE = 0.02
F32 = jnp.float32
BF16 = jnp.bfloat16
VMEM = pl.BlockSpec(memory_space=pltpu.VMEM)
SMEM = pl.BlockSpec(memory_space=pltpu.SMEM)
PARAMS = pltpu.CompilerParams(vmem_limit_bytes=48 * 1024 * 1024)


def make_tables(side):
    ordinal = np.arange(side, dtype=np.int64)
    angles = -2.0 * math.pi / side * (ordinal[:, None] * ordinal[None, :] % side)
    transform = np.exp(1j * angles) / math.sqrt(side)
    frequency = (ordinal + side // 2) % side - side // 2
    phases = np.exp(-0.25j * math.pi / side * frequency**2)
    spread = transform.conj() @ (phases[:, None] * transform)
    tables = []
    for matrix in (transform, spread):
        block = np.block([[matrix.real, matrix.imag], [-matrix.imag, matrix.real]])
        for part in (block, block.T):
            high = part.astype(np.float32).astype(ml_dtypes.bfloat16)
            low = (part - high.astype(np.float64)).astype(np.float32).astype(ml_dtypes.bfloat16)
            tables += [high, low]
    return np.stack(tables)


def split(values):
    high = values.astype(BF16)
    return high, (values - high.astype(F32)).astype(BF16)


def dot(left, right):
    return jnp.dot(left, right, preferred_element_type=F32)


def right_mul(field, table):
    high, low = table
    deep = jnp.concatenate([high[...], high[...], low[...]], axis=0)
    reals, imags = [], []
    for real, imag in zip(*field):
        side = real.shape[0]
        x_high, x_low = split(jnp.concatenate([real, imag], axis=1))
        out = dot(jnp.concatenate([x_high, x_low, x_high], axis=1), deep)
        reals.append(out[:, :side])
        imags.append(out[:, side:])
    return reals, imags


def left_mul(field, table):
    high, low = table
    reals, imags = [], []
    for real, imag in zip(*field):
        side = real.shape[0]
        x_high, x_low = split(jnp.concatenate([real, imag], axis=0))
        wide = dot(high[...], jnp.concatenate([x_high, x_low], axis=1))
        out = wide[:, :side] + wide[:, side:] + dot(low[...], x_high)
        reals.append(out[:side])
        imags.append(out[side:])
    return reals, imags


def both_mul(field, table, turned):
    return left_mul(right_mul(field, table), turned)


def times(a, b):
    return (
        [x * u - y * v for x, y, u, v in zip(a[0], a[1], b[0], b[1])],
        [x * v + y * u for x, y, u, v in zip(a[0], a[1], b[0], b[1])],
    )


def conj_times(a, b):
    return (
        [x * u + y * v for x, y, u, v in zip(a[0], a[1], b[0], b[1])],
        [x * v - y * u for x, y, u, v in zip(a[0], a[1], b[0], b[1])],
    )


def lanes(shape):
    return lax.broadcasted_iota(jnp.int32, shape, len(shape) - 1)


def halves(side, flipped):
    return (lanes((side, side)) < side // 2) != flipped


def odd_column():
    return lax.rem(lax.axis_index("col"), 2) == 1


def pack_body(tile, near, far):
    layers, _, side, _ = tile.shape
    pick = halves(side, odd_column())
    for s in range(layers):
        real, turned = tile[s, 0], pltpu.roll(tile[s, 1], side // 2, 1)
        near[s] = jnp.where(pick, real, turned)
        far[s] = jnp.where(pick, turned, real)


def odd_row():
    return lax.rem(lax.axis_index("row"), 2) == 1


def rows_out(blocks, s, c, near, far, half):
    odd = odd_row()
    for k, block in enumerate(blocks):
        near[k, s, c] = jnp.where(odd, block[half:], block[:half])
        far[k, s, c] = jnp.where(odd, block[:half], block[half:])


def halo_body(tile, near, far, side_block, to_below, to_above):
    layers, _, side, _ = tile.shape
    half = side // 2
    pick = halves(side, odd_column())
    for s in range(layers):
        parts = jnp.where(pick, far[s], near[s]), pltpu.roll(jnp.where(pick, near[s], far[s]), half, 1)
        for c in range(2):
            side_block[s, c] = parts[c]
            rows_out((tile[s, c], parts[c]), s, c, to_below, to_above, half)


def slots_body(
    places, tile, side_block, from_above, from_below, probe, measured,
    tables, grad_tile, grad_side, to_below, to_above, turning, windows, incident,
):
    layers, _, side, _ = tile.shape
    half = side // 2
    slots = measured.shape[2]
    row = lax.broadcasted_iota(jnp.int32, (side, side), 0)
    lane = lax.broadcasted_iota(jnp.int32, (side, side), 1)
    row_in, lane_in, row_back, row_fwd, lane_back, lane_fwd = [], [], [], [], [], []
    for j in range(slots):
        p, q = places[2 * j] - half, places[2 * j + 1] - half
        row_in.append((row >= p) & (row < p + side))
        lane_in.append((lane >= q) & (lane < q + side))
        row_back.append(lax.rem(p + side, side))
        row_fwd.append(lax.rem(side - p, side))
        lane_back.append(lax.rem(side - q, side))
        lane_fwd.append(lax.rem(q + side, side))
    odd = odd_row()

    def cut(s):
        for c in range(2):
            row_block, both_block = [
                jnp.concatenate(
                    [
                        jnp.where(odd, from_above[k, s, c], from_below[k, s, c]),
                        jnp.where(odd, from_below[k, s, c], from_above[k, s, c]),
                    ],
                    axis=0,
                )
                for k in range(2)
            ]
            for j in range(slots):
                inner = jnp.where(lane_in[j], tile[s, c], side_block[s, c])
                outer = jnp.where(lane_in[j], row_block, both_block)
                mixed = pltpu.roll(jnp.where(row_in[j], inner, outer), lane_back[j], 1)
                place = turning.at[(s * 2 + c) * slots + j]
                place[:side] = mixed
                place[side:] = mixed
                windows[s, c, j] = place[pl.ds(row_back[j], side), :]

    def layer(s):
        return [windows[s, 0, j] for j in range(slots)], [windows[s, 1, j] for j in range(slots)]

    def incoming(s):
        if s == 0:
            return [probe[0]] * slots, [probe[1]] * slots
        return [incident[s - 1, 0, j] for j in range(slots)], [
            incident[s - 1, 1, j] for j in range(slots)
        ]

    fwd, inv, on, off = [(tables.at[2 * k], tables.at[2 * k + 1]) for k in range(4)]
    cut(0)
    for s in range(layers):
        wave = times(layer(s), incoming(s))
        if s + 1 < layers:
            cut(s + 1)
            wave = both_mul(wave, on, off)
            for c in range(2):
                for j in range(slots):
                    incident[s, c, j] = wave[c][j]
    far = both_mul(wave, fwd, inv)
    residue = [
        far[0][j] * far[0][j] + far[1][j] * far[1][j] - measured[0, 0, j] for j in range(slots)
    ]
    back = ([a * b for a, b in zip(residue, far[0])], [a * b for a, b in zip(residue, far[1])])
    back = both_mul(back, inv, fwd)
    for s in reversed(range(layers)):
        product = conj_times(incoming(s), back)
        for c in range(2):
            moved = []
            for j in range(slots):
                turned = pltpu.roll(product[c][j], lane_fwd[j], 1)
                place = turning.at[(s * 2 + c) * slots + j]
                place[:side] = turned
                place[side:] = turned
                live = j < places[2 * slots]
                moved.append(jnp.where(live, place[pl.ds(row_fwd[j], side), :], 0.0))

            def total(rows_of, lanes_of):
                terms = [
                    jnp.where(rows_of(row_in[j]) & lanes_of(lane_in[j]), moved[j], 0.0)
                    for j in range(slots)
                ]
                return functools.reduce(lambda a, b: a + b, terms)

            same, other = (lambda m: m), (lambda m: ~m)
            grad_tile[s, c] = total(same, same)
            grad_side[s, c] = total(same, other)
            for k, lanes_of in enumerate((same, other)):
                block = total(other, lanes_of)
                to_below[k, s, c] = jnp.where(odd, block[:half], block[half:])
                to_above[k, s, c] = jnp.where(odd, block[half:], block[:half])
        if s > 0:
            back = both_mul(conj_times(layer(s), back), off, on)


def joined_rows(grad, k, from_above, from_below, s, c):
    odd, near, far = odd_row(), from_above[k, s, c], from_below[k, s, c]
    return grad[s, c] + jnp.concatenate([jnp.where(odd, far, near), jnp.where(odd, near, far)], axis=0)


def middle_body(grad_tile, grad_side, from_above, from_below, new_tile, new_side, near, far):
    layers, _, side, _ = grad_tile.shape
    pick = halves(side, odd_column())
    for s in range(layers):
        for c in range(2):
            inner = joined_rows(grad_tile, 0, from_above, from_below, s, c)
            outer = joined_rows(grad_side, 1, from_above, from_below, s, c)
            new_tile[s, c] = inner
            new_side[s, c] = outer
            near[s, c] = jnp.where(pick, inner, outer)
            far[s, c] = jnp.where(pick, outer, inner)


def step_body(
    tile, side_block, grad_tile, grad_side, near, far, new_tile, new_side, to_below, to_above
):
    layers, _, side, _ = tile.shape
    half = side // 2
    pick = halves(side, odd_column())
    col, cols = lax.axis_index("col"), lax.axis_size("col")
    lane = lanes((side, side))
    first = jnp.where(col + 1 < cols, 0, half)
    last = jnp.where(col > 0, side, half)
    on_grid = (lane >= first) & (lane < last)
    for s in range(layers):
        for c in range(2):
            inner = grad_tile[s, c] + jnp.where(pick, near[s, c], far[s, c])
            outer = grad_side[s, c] + jnp.where(pick, far[s, c], near[s, c])
            inner = tile[s, c] - LEARNING_RATE * inner
            outer = jnp.where(on_grid, side_block[s, c] - LEARNING_RATE * outer, 0.0)
            new_tile[s, c] = inner
            new_side[s, c] = outer
            rows_out((inner, outer), s, c, to_below, to_above, half)


def last_rows_body(grad_tile, grad_side, from_above, from_below, new_tile, near, far):
    layers, _, side, _ = grad_tile.shape
    half = side // 2
    pick = halves(side, odd_column())
    for s in range(layers):
        outer = []
        for c in range(2):
            new_tile[s, c] = joined_rows(grad_tile, 0, from_above, from_below, s, c)
            outer.append(joined_rows(grad_side, 1, from_above, from_below, s, c))
        turned = pltpu.roll(outer[1], half, 1)
        near[s] = jnp.where(pick, turned, outer[0])
        far[s] = jnp.where(pick, outer[0], turned)


def last_body(tile, grad_tile, near, far, out):
    layers, _, side, _ = tile.shape
    half = side // 2
    pick = halves(side, odd_column())
    for s in range(layers):
        real = jnp.where(pick, near[s], far[s])
        imag = pltpu.roll(jnp.where(pick, far[s], near[s]), half, 1)
        for c, part in enumerate((real, imag)):
            out[s, c] = tile[s, c] - LEARNING_RATE * (grad_tile[s, c] + part)


def call(body, shapes, *operands, specs=None, scratch=(), name=None, flops=0):
    return pl.pallas_call(
        body,
        out_shape=[jax.ShapeDtypeStruct(shape, F32) for shape in shapes],
        in_specs=specs or [VMEM] * len(operands),
        out_specs=[VMEM] * len(shapes),
        scratch_shapes=list(scratch),
        compiler_params=PARAMS,
        name=name,
        cost_estimate=pl.CostEstimate(
            flops=flops,
            bytes_accessed=sum(4 * math.prod(shape) for shape in shapes),
            transcendentals=0,
        ),
    )(*operands)


def across(axis, near, far):
    count = lax.axis_size(axis)
    trades = []
    for block, start in ((near, 1), (far, 0)):
        pairs = [(i, i + 1) for i in range(start, count - 1, 2)]
        trades.append(lax.ppermute(block, axis, pairs + [(j, i) for i, j in pairs]))
    return trades


def shards(object_field, probe, measured, positions, counts):
    layers, _, side, _ = object_field.shape
    half = side // 2
    slots = positions.shape[2]
    places = jnp.concatenate([positions.reshape(2 * slots), counts.reshape(1)])
    tables = jnp.where(counts[0, 0] > 0, jnp.asarray(make_tables(side)), 0)
    whole, packed, strips = (layers, 2, side, side), (layers, side, side), (2, layers, 2, half, side)
    scratch = (
        pltpu.VMEM((layers * 2 * slots, 2 * side, side), F32),
        pltpu.VMEM((layers, 2, slots, side, side), F32),
        pltpu.VMEM((layers - 1, 2, slots, side, side), F32),
    )
    products = 2 * layers
    flops = products * 2 * 3 * 2 * (2 * side) ** 2 * (slots * side)
    tile = object_field
    sent = call(pack_body, (packed, packed), tile, name="pack")
    side_block, *sent = call(
        halo_body, (whole, strips, strips), tile, *across("col", *sent), name="halo"
    )
    for iteration in range(ITERS):
        from_above, from_below = across("row", *sent)
        grad_tile, grad_side, *sent = call(
            slots_body,
            (whole, whole, strips, strips),
            places, tile, side_block, from_above, from_below, probe, measured, tables,
            specs=[SMEM] + [VMEM] * 7,
            scratch=scratch,
            name="slots",
            flops=flops,
        )
        from_above, from_below = across("row", *sent)
        if iteration + 1 < ITERS:
            grad_tile, grad_side, *sent = call(
                middle_body, (whole, whole, whole, whole), grad_tile, grad_side, from_above, from_below, name="middle"
            )
            tile, side_block, *sent = call(
                step_body,
                (whole, whole, strips, strips),
                tile, side_block, grad_tile, grad_side, *across("col", *sent),
                name="step",
            )
        else:
            grad_tile, *sent = call(
                last_rows_body, (whole, packed, packed), grad_tile, grad_side, from_above, from_below, name="last_rows"
            )
            (tile,) = call(last_body, (whole,), tile, grad_tile, *across("col", *sent), name="last")
    return tile


def solution(mesh):
    placed = (
        P(None, None, "row", "col"),
        P(),
        P("row", "col", None, None, None),
        P("row", "col", None, None),
        P("row", "col"),
    )
    return jax.shard_map(
        shards, mesh=mesh, in_specs=placed, out_specs=P(None, None, "row", "col"), check_vma=False
    )
```

```python
import functools
import math

import jax
import jax.numpy as jnp
import ml_dtypes
import numpy as np
from jax import lax
from jax.experimental import pallas as pl
from jax.experimental.pallas import tpu as pltpu
from jax.sharding import PartitionSpec as P

ITERS = 2
LEARNING_RATE = 0.02
F32 = jnp.float32
BF16 = jnp.bfloat16
VMEM = pl.BlockSpec(memory_space=pltpu.VMEM)
SMEM = pl.BlockSpec(memory_space=pltpu.SMEM)
ANY = pl.BlockSpec(memory_space=pl.ANY)
PARAMS = pltpu.CompilerParams(vmem_limit_bytes=48 * 1024 * 1024)


def make_tables(side):
    ordinal = np.arange(side, dtype=np.int64)
    angles = -2.0 * math.pi / side * (ordinal[:, None] * ordinal[None, :] % side)
    transform = np.exp(1j * angles) / math.sqrt(side)
    frequency = (ordinal + side // 2) % side - side // 2
    phases = np.exp(-0.25j * math.pi / side * frequency**2)
    spread = transform.conj() @ (phases[:, None] * transform)
    tables = []
    for matrix in (transform, spread):
        block = np.block([[matrix.real, matrix.imag], [-matrix.imag, matrix.real]])
        for part in (block, block.T):
            high = part.astype(np.float32).astype(ml_dtypes.bfloat16)
            low = (part - high.astype(np.float64)).astype(np.float32).astype(ml_dtypes.bfloat16)
            tables += [high, low]
    return np.stack(tables)


def split(values):
    high = values.astype(BF16)
    return high, (values - high.astype(F32)).astype(BF16)


def dot(left, right):
    return jnp.dot(left, right, preferred_element_type=F32)


def right_mul(field, table):
    high, low = table
    deep = jnp.concatenate([high[...], high[...], low[...]], axis=0)
    reals, imags = [], []
    for real, imag in zip(*field):
        side = real.shape[0]
        x_high, x_low = split(jnp.concatenate([real, imag], axis=1))
        out = dot(jnp.concatenate([x_high, x_low, x_high], axis=1), deep)
        reals.append(out[:, :side])
        imags.append(out[:, side:])
    return reals, imags


def left_mul(field, table):
    high, low = table
    reals, imags = [], []
    for real, imag in zip(*field):
        side = real.shape[0]
        x_high, x_low = split(jnp.concatenate([real, imag], axis=0))
        wide = dot(high[...], jnp.concatenate([x_high, x_low], axis=1))
        out = wide[:, :side] + wide[:, side:] + dot(low[...], x_high)
        reals.append(out[:side])
        imags.append(out[side:])
    return reals, imags


def both_mul(field, table, turned):
    return left_mul(right_mul(field, table), turned)


def times(a, b):
    return (
        [x * u - y * v for x, y, u, v in zip(a[0], a[1], b[0], b[1])],
        [x * v + y * u for x, y, u, v in zip(a[0], a[1], b[0], b[1])],
    )


def conj_times(a, b):
    return (
        [x * u + y * v for x, y, u, v in zip(a[0], a[1], b[0], b[1])],
        [x * v - y * u for x, y, u, v in zip(a[0], a[1], b[0], b[1])],
    )


def lanes(shape):
    return lax.broadcasted_iota(jnp.int32, shape, len(shape) - 1)


def halves(side, flipped):
    return (lanes((side, side)) < side // 2) != flipped


def odd_column():
    return lax.rem(lax.axis_index("col"), 2) == 1


def pack_body(tile, near, far):
    layers, _, side, _ = tile.shape
    pick = halves(side, odd_column())
    for s in range(layers):
        real, turned = tile[s, 0], pltpu.roll(tile[s, 1], side // 2, 1)
        near[s] = jnp.where(pick, real, turned)
        far[s] = jnp.where(pick, turned, real)


def odd_row():
    return lax.rem(lax.axis_index("row"), 2) == 1


def rows_out(blocks, s, c, near, far, half):
    odd = odd_row()
    for k, block in enumerate(blocks):
        near[k, s, c] = jnp.where(odd, block[half:], block[:half])
        far[k, s, c] = jnp.where(odd, block[:half], block[half:])


def halo_body(tile, near, far, side_block, to_below, to_above):
    layers, _, side, _ = tile.shape
    half = side // 2
    pick = halves(side, odd_column())
    for s in range(layers):
        parts = jnp.where(pick, far[s], near[s]), pltpu.roll(jnp.where(pick, near[s], far[s]), half, 1)
        for c in range(2):
            side_block[s, c] = parts[c]
            rows_out((tile[s, c], parts[c]), s, c, to_below, to_above, half)


def footprints(places, slots, side):
    row = lax.broadcasted_iota(jnp.int32, (side, side), 0)
    lane = lax.broadcasted_iota(jnp.int32, (side, side), 1)
    row_in, lane_in = [], []
    for j in range(slots):
        p, q = places[2 * j] - side // 2, places[2 * j + 1] - side // 2
        row_in.append((row >= p) & (row < p + side))
        lane_in.append((lane >= q) & (lane < q + side))
    return row_in, lane_in


def covered(moved, row_in, lane_in, own_rows, own_lanes):
    terms = [
        jnp.where((r if own_rows else ~r) & (l if own_lanes else ~l), block, 0.0)
        for block, r, l in zip(moved, row_in, lane_in)
    ]
    return functools.reduce(lambda a, b: a + b, terms)


def keep_body(places, gradients, grad_tile, grad_side):
    layers, _, slots, side, _ = gradients.shape
    row_in, lane_in = footprints(places, slots, side)
    for s in range(layers):
        for c in range(2):
            moved = [gradients[s, c, j] for j in range(slots)]
            grad_tile[s, c] = covered(moved, row_in, lane_in, True, True)
            grad_side[s, c] = covered(moved, row_in, lane_in, True, False)


def slots_body(
    places, tile, side_block, from_above, from_below, probe, measured,
    tables, gradients, to_below, to_above, turning, windows, incident,
):
    layers, _, side, _ = tile.shape
    half = side // 2
    slots = measured.shape[2]
    row_in, lane_in = footprints(places, slots, side)
    row_back, row_fwd, lane_back, lane_fwd = [], [], [], []
    for j in range(slots):
        p, q = places[2 * j] - half, places[2 * j + 1] - half
        row_back.append(lax.rem(p + side, side))
        row_fwd.append(lax.rem(side - p, side))
        lane_back.append(lax.rem(side - q, side))
        lane_fwd.append(lax.rem(q + side, side))
    odd = odd_row()

    def cut(s):
        for c in range(2):
            row_block, both_block = [
                jnp.concatenate(
                    [
                        jnp.where(odd, from_above[k, s, c], from_below[k, s, c]),
                        jnp.where(odd, from_below[k, s, c], from_above[k, s, c]),
                    ],
                    axis=0,
                )
                for k in range(2)
            ]
            for j in range(slots):
                inner = jnp.where(lane_in[j], tile[s, c], side_block[s, c])
                outer = jnp.where(lane_in[j], row_block, both_block)
                mixed = pltpu.roll(jnp.where(row_in[j], inner, outer), lane_back[j], 1)
                place = turning.at[(s * 2 + c) * slots + j]
                place[:side] = mixed
                place[side:] = mixed
                windows[s, c, j] = place[pl.ds(row_back[j], side), :]

    def layer(s):
        return [windows[s, 0, j] for j in range(slots)], [windows[s, 1, j] for j in range(slots)]

    def incoming(s):
        if s == 0:
            return [probe[0]] * slots, [probe[1]] * slots
        return [incident[s - 1, 0, j] for j in range(slots)], [
            incident[s - 1, 1, j] for j in range(slots)
        ]

    fwd, inv, on, off = [(tables.at[2 * k], tables.at[2 * k + 1]) for k in range(4)]
    cut(0)
    for s in range(layers):
        wave = times(layer(s), incoming(s))
        if s + 1 < layers:
            cut(s + 1)
            wave = both_mul(wave, on, off)
            for c in range(2):
                for j in range(slots):
                    incident[s, c, j] = wave[c][j]
    far = both_mul(wave, fwd, inv)
    residue = [
        far[0][j] * far[0][j] + far[1][j] * far[1][j] - measured[0, 0, j] for j in range(slots)
    ]
    back = ([a * b for a, b in zip(residue, far[0])], [a * b for a, b in zip(residue, far[1])])
    back = both_mul(back, inv, fwd)
    for s in reversed(range(layers)):
        product = conj_times(incoming(s), back)
        for c in range(2):
            moved = []
            for j in range(slots):
                turned = pltpu.roll(product[c][j], lane_fwd[j], 1)
                place = turning.at[(s * 2 + c) * slots + j]
                place[:side] = turned
                place[side:] = turned
                live = j < places[2 * slots]
                moved.append(jnp.where(live, place[pl.ds(row_fwd[j], side), :], 0.0))

            for j in range(slots):
                gradients[s, c, j] = moved[j]
            for k in range(2):
                block = covered(moved, row_in, lane_in, False, k == 0)
                to_below[k, s, c] = jnp.where(odd, block[:half], block[half:])
                to_above[k, s, c] = jnp.where(odd, block[half:], block[:half])
        if s > 0:
            back = both_mul(conj_times(layer(s), back), off, on)


def joined_rows(grad, k, from_above, from_below, s, c):
    odd, near, far = odd_row(), from_above[k, s, c], from_below[k, s, c]
    return grad[s, c] + jnp.concatenate([jnp.where(odd, far, near), jnp.where(odd, near, far)], axis=0)


def middle_body(grad_tile, grad_side, from_above, from_below, new_tile, new_side, near, far):
    layers, _, side, _ = grad_tile.shape
    pick = halves(side, odd_column())
    for s in range(layers):
        for c in range(2):
            inner = joined_rows(grad_tile, 0, from_above, from_below, s, c)
            outer = joined_rows(grad_side, 1, from_above, from_below, s, c)
            new_tile[s, c] = inner
            new_side[s, c] = outer
            near[s, c] = jnp.where(pick, inner, outer)
            far[s, c] = jnp.where(pick, outer, inner)


def step_body(
    tile, side_block, grad_tile, grad_side, near, far, new_tile, new_side, to_below, to_above
):
    layers, _, side, _ = tile.shape
    half = side // 2
    pick = halves(side, odd_column())
    col, cols = lax.axis_index("col"), lax.axis_size("col")
    lane = lanes((side, side))
    first = jnp.where(col + 1 < cols, 0, half)
    last = jnp.where(col > 0, side, half)
    on_grid = (lane >= first) & (lane < last)
    for s in range(layers):
        for c in range(2):
            inner = grad_tile[s, c] + jnp.where(pick, near[s, c], far[s, c])
            outer = grad_side[s, c] + jnp.where(pick, far[s, c], near[s, c])
            inner = tile[s, c] - LEARNING_RATE * inner
            outer = jnp.where(on_grid, side_block[s, c] - LEARNING_RATE * outer, 0.0)
            new_tile[s, c] = inner
            new_side[s, c] = outer
            rows_out((inner, outer), s, c, to_below, to_above, half)


def last_rows_body(grad_tile, grad_side, from_above, from_below, new_tile, near, far):
    layers, _, side, _ = grad_tile.shape
    half = side // 2
    pick = halves(side, odd_column())
    for s in range(layers):
        outer = []
        for c in range(2):
            new_tile[s, c] = joined_rows(grad_tile, 0, from_above, from_below, s, c)
            outer.append(joined_rows(grad_side, 1, from_above, from_below, s, c))
        turned = pltpu.roll(outer[1], half, 1)
        near[s] = jnp.where(pick, turned, outer[0])
        far[s] = jnp.where(pick, outer[0], turned)


def last_body(tile, grad_tile, near, far, out, held, sems):
    layers, _, side, _ = tile.shape
    pick = halves(side, odd_column())
    copies = [pltpu.make_async_copy(held.at[s], out.at[s], sems.at[s]) for s in range(layers)]
    for s in range(layers):
        imag = pltpu.roll(jnp.where(pick, far[s], near[s]), side // 2, 1)
        for c, part in enumerate((jnp.where(pick, near[s], far[s]), imag)):
            held[s, c] = tile[s, c] - LEARNING_RATE * (grad_tile[s, c] + part)
        copies[s].start()
    for copy in copies:
        copy.wait()


def call(body, shapes, *operands, specs=None, outs=None, scratch=(), name=None, flops=0):
    return pl.pallas_call(
        body,
        out_shape=[jax.ShapeDtypeStruct(shape, F32) for shape in shapes],
        in_specs=specs or [VMEM] * len(operands),
        out_specs=outs or [VMEM] * len(shapes),
        scratch_shapes=list(scratch),
        compiler_params=PARAMS,
        name=name,
        cost_estimate=pl.CostEstimate(
            flops=flops,
            bytes_accessed=sum(4 * math.prod(shape) for shape in shapes),
            transcendentals=0,
        ),
    )(*operands)


def across(axis, near, far):
    count = lax.axis_size(axis)
    trades = []
    for block, start in ((near, 1), (far, 0)):
        pairs = [(i, i + 1) for i in range(start, count - 1, 2)]
        trades.append(lax.ppermute(block, axis, pairs + [(j, i) for i, j in pairs]))
    return trades


def shards(object_field, probe, measured, positions, counts):
    layers, _, side, _ = object_field.shape
    half = side // 2
    slots = positions.shape[2]
    places = jnp.concatenate([positions.reshape(2 * slots), counts.reshape(1)])
    tables = jnp.where(counts[0, 0] > 0, jnp.asarray(make_tables(side)), 0)
    whole, packed, strips = (layers, 2, side, side), (layers, side, side), (2, layers, 2, half, side)
    scratch = (
        pltpu.VMEM((layers * 2 * slots, 2 * side, side), F32),
        pltpu.VMEM((layers, 2, slots, side, side), F32),
        pltpu.VMEM((layers - 1, 2, slots, side, side), F32),
    )
    products = 2 * layers
    flops = products * 2 * 3 * 2 * (2 * side) ** 2 * (slots * side)
    tile = object_field
    held = (pltpu.VMEM(whole, F32), pltpu.SemaphoreType.DMA((layers,)))
    sent = call(pack_body, (packed, packed), tile, name="pack")
    side_block, *sent = call(
        halo_body, (whole, strips, strips), tile, *across("col", *sent), name="halo"
    )
    for iteration in range(ITERS):
        from_above, from_below = across("row", *sent)
        parts, *sent = call(
            slots_body,
            ((layers, 2, slots, side, side), strips, strips),
            places, tile, side_block, from_above, from_below, probe, measured, tables,
            specs=[SMEM] + [VMEM] * 7,
            scratch=scratch,
            name="slots",
            flops=flops,
        )
        grad_tile, grad_side = call(
            keep_body, (whole, whole), places, parts, specs=[SMEM, VMEM], name="keep"
        )
        from_above, from_below = across("row", *sent)
        if iteration + 1 < ITERS:
            grad_tile, grad_side, *sent = call(
                middle_body, (whole, whole, whole, whole), grad_tile, grad_side, from_above, from_below, name="middle"
            )
            tile, side_block, *sent = call(
                step_body,
                (whole, whole, strips, strips),
                tile, side_block, grad_tile, grad_side, *across("col", *sent),
                name="step",
            )
        else:
            grad_tile, *sent = call(
                last_rows_body, (whole, packed, packed), grad_tile, grad_side, from_above, from_below, name="last_rows"
            )
            (tile,) = call(
                last_body, (whole,), tile, grad_tile, *across("col", *sent), outs=[ANY], scratch=held, name="last"
            )
    return tile


def solution(mesh):
    placed = (
        P(None, None, "row", "col"),
        P(),
        P("row", "col", None, None, None),
        P("row", "col", None, None),
        P("row", "col"),
    )
    return jax.shard_map(
        shards, mesh=mesh, in_specs=placed, out_specs=P(None, None, "row", "col"), check_vma=False
    )
```

```python
import functools
import math

import jax
import jax.numpy as jnp
import ml_dtypes
import numpy as np
from jax import lax
from jax.experimental import pallas as pl
from jax.experimental.pallas import tpu as pltpu
from jax.sharding import PartitionSpec as P

ITERS = 2
LEARNING_RATE = 0.02
F32 = jnp.float32
BF16 = jnp.bfloat16
VMEM = pl.BlockSpec(memory_space=pltpu.VMEM)
SMEM = pl.BlockSpec(memory_space=pltpu.SMEM)
ANY = pl.BlockSpec(memory_space=pl.ANY)
PARAMS = pltpu.CompilerParams(vmem_limit_bytes=48 * 1024 * 1024)


def make_tables(side):
    ordinal = np.arange(side, dtype=np.int64)
    angles = -2.0 * math.pi / side * (ordinal[:, None] * ordinal[None, :] % side)
    transform = np.exp(1j * angles) / math.sqrt(side)
    frequency = (ordinal + side // 2) % side - side // 2
    phases = np.exp(-0.25j * math.pi / side * frequency**2)
    spread = transform.conj() @ (phases[:, None] * transform)
    tables = []
    for matrix in (transform, spread):
        block = np.block([[matrix.real, matrix.imag], [-matrix.imag, matrix.real]])
        for part in (block, block.T):
            high = part.astype(np.float32).astype(ml_dtypes.bfloat16)
            low = (part - high.astype(np.float64)).astype(np.float32).astype(ml_dtypes.bfloat16)
            tables += [high, low]
    return np.stack(tables)


def split(values):
    high = values.astype(BF16)
    return high, (values - high.astype(F32)).astype(BF16)


def dot(left, right):
    return jnp.dot(left, right, preferred_element_type=F32)


def right_mul(field, table):
    high, low = table
    deep = jnp.concatenate([high[...], high[...], low[...]], axis=0)
    reals, imags = [], []
    for real, imag in zip(*field):
        side = real.shape[0]
        x_high, x_low = split(jnp.concatenate([real, imag], axis=1))
        out = dot(jnp.concatenate([x_high, x_low, x_high], axis=1), deep)
        reals.append(out[:, :side])
        imags.append(out[:, side:])
    return reals, imags


def left_mul(field, table):
    high, low = table
    reals, imags = [], []
    for real, imag in zip(*field):
        side = real.shape[0]
        x_high, x_low = split(jnp.concatenate([real, imag], axis=0))
        wide = dot(high[...], jnp.concatenate([x_high, x_low], axis=1))
        out = wide[:, :side] + wide[:, side:] + dot(low[...], x_high)
        reals.append(out[:side])
        imags.append(out[side:])
    return reals, imags


def both_mul(field, table, turned):
    return left_mul(right_mul(field, table), turned)


def times(a, b):
    return (
        [x * u - y * v for x, y, u, v in zip(a[0], a[1], b[0], b[1])],
        [x * v + y * u for x, y, u, v in zip(a[0], a[1], b[0], b[1])],
    )


def conj_times(a, b):
    return (
        [x * u + y * v for x, y, u, v in zip(a[0], a[1], b[0], b[1])],
        [x * v - y * u for x, y, u, v in zip(a[0], a[1], b[0], b[1])],
    )


def lanes(shape):
    return lax.broadcasted_iota(jnp.int32, shape, len(shape) - 1)


def halves(side, flipped):
    return (lanes((side, side)) < side // 2) != flipped


def odd_column():
    return lax.rem(lax.axis_index("col"), 2) == 1


def pack_body(tile, near, far):
    side = near.shape[-1]
    pick = halves(side, odd_column())
    real, turned = tile[0, 0], pltpu.roll(tile[0, 1], side // 2, 1)
    near[0] = jnp.where(pick, real, turned)
    far[0] = jnp.where(pick, turned, real)


def odd_row():
    return lax.rem(lax.axis_index("row"), 2) == 1


def rows_out(blocks, s, c, near, far, half):
    odd = odd_row()
    for k, block in enumerate(blocks):
        near[k, s, c] = jnp.where(odd, block[half:], block[:half])
        far[k, s, c] = jnp.where(odd, block[:half], block[half:])


def halo_body(tile, near, far, side_block, to_below, to_above):
    layers, _, side, _ = tile.shape
    half = side // 2
    pick = halves(side, odd_column())
    for s in range(layers):
        parts = jnp.where(pick, far[s], near[s]), pltpu.roll(jnp.where(pick, near[s], far[s]), half, 1)
        for c in range(2):
            side_block[s, c] = parts[c]
            rows_out((tile[s, c], parts[c]), s, c, to_below, to_above, half)


def footprints(places, slots, side):
    row = lax.broadcasted_iota(jnp.int32, (side, side), 0)
    lane = lax.broadcasted_iota(jnp.int32, (side, side), 1)
    row_in, lane_in = [], []
    for j in range(slots):
        p, q = places[2 * j] - side // 2, places[2 * j + 1] - side // 2
        row_in.append((row >= p) & (row < p + side))
        lane_in.append((lane >= q) & (lane < q + side))
    return row_in, lane_in


def covered(moved, row_in, lane_in, own_rows, own_lanes):
    terms = [
        jnp.where((r if own_rows else ~r) & (l if own_lanes else ~l), block, 0.0)
        for block, r, l in zip(moved, row_in, lane_in)
    ]
    return functools.reduce(lambda a, b: a + b, terms)


def keep_body(places, gradients, grad_tile, grad_side):
    layers, _, slots, side, _ = gradients.shape
    row_in, lane_in = footprints(places, slots, side)
    for s in range(layers):
        for c in range(2):
            moved = [gradients[s, c, j] for j in range(slots)]
            grad_tile[s, c] = covered(moved, row_in, lane_in, True, True)
            grad_side[s, c] = covered(moved, row_in, lane_in, True, False)


def slots_body(
    places, tile, side_block, from_above, from_below, probe, measured,
    tables, gradients, to_below, to_above, turning, windows, incident,
):
    layers, _, side, _ = tile.shape
    half = side // 2
    slots = measured.shape[2]
    row_in, lane_in = footprints(places, slots, side)
    row_back, row_fwd, lane_back, lane_fwd = [], [], [], []
    for j in range(slots):
        p, q = places[2 * j] - half, places[2 * j + 1] - half
        row_back.append(lax.rem(p + side, side))
        row_fwd.append(lax.rem(side - p, side))
        lane_back.append(lax.rem(side - q, side))
        lane_fwd.append(lax.rem(q + side, side))
    odd = odd_row()

    def cut(s):
        for c in range(2):
            row_block, both_block = [
                jnp.concatenate(
                    [
                        jnp.where(odd, from_above[k, s, c], from_below[k, s, c]),
                        jnp.where(odd, from_below[k, s, c], from_above[k, s, c]),
                    ],
                    axis=0,
                )
                for k in range(2)
            ]
            for j in range(slots):
                inner = jnp.where(lane_in[j], tile[s, c], side_block[s, c])
                outer = jnp.where(lane_in[j], row_block, both_block)
                mixed = pltpu.roll(jnp.where(row_in[j], inner, outer), lane_back[j], 1)
                place = turning.at[(s * 2 + c) * slots + j]
                place[:side] = mixed
                place[side:] = mixed
                windows[s, c, j] = place[pl.ds(row_back[j], side), :]

    def layer(s):
        return [windows[s, 0, j] for j in range(slots)], [windows[s, 1, j] for j in range(slots)]

    def incoming(s):
        if s == 0:
            return [probe[0]] * slots, [probe[1]] * slots
        return [incident[s - 1, 0, j] for j in range(slots)], [
            incident[s - 1, 1, j] for j in range(slots)
        ]

    fwd, inv, on, off = [(tables.at[2 * k], tables.at[2 * k + 1]) for k in range(4)]
    cut(0)
    for s in range(layers):
        wave = times(layer(s), incoming(s))
        if s + 1 < layers:
            cut(s + 1)
            wave = both_mul(wave, on, off)
            for c in range(2):
                for j in range(slots):
                    incident[s, c, j] = wave[c][j]
    far = both_mul(wave, fwd, inv)
    residue = [
        far[0][j] * far[0][j] + far[1][j] * far[1][j] - measured[0, 0, j] for j in range(slots)
    ]
    back = ([a * b for a, b in zip(residue, far[0])], [a * b for a, b in zip(residue, far[1])])
    back = both_mul(back, inv, fwd)
    for s in reversed(range(layers)):
        product = conj_times(incoming(s), back)
        for c in range(2):
            moved = []
            for j in range(slots):
                turned = pltpu.roll(product[c][j], lane_fwd[j], 1)
                place = turning.at[(s * 2 + c) * slots + j]
                place[:side] = turned
                place[side:] = turned
                live = j < places[2 * slots]
                moved.append(jnp.where(live, place[pl.ds(row_fwd[j], side), :], 0.0))

            for j in range(slots):
                gradients[s, c, j] = moved[j]
            for k in range(2):
                block = covered(moved, row_in, lane_in, False, k == 0)
                to_below[k, s, c] = jnp.where(odd, block[:half], block[half:])
                to_above[k, s, c] = jnp.where(odd, block[half:], block[:half])
        if s > 0:
            back = both_mul(conj_times(layer(s), back), off, on)


def joined_rows(grad, k, from_above, from_below, s, c):
    odd, near, far = odd_row(), from_above[k, s, c], from_below[k, s, c]
    return grad[s, c] + jnp.concatenate([jnp.where(odd, far, near), jnp.where(odd, near, far)], axis=0)


def middle_body(grad_tile, grad_side, from_above, from_below, new_tile, new_side, near, far):
    layers, _, side, _ = grad_tile.shape
    pick = halves(side, odd_column())
    for s in range(layers):
        for c in range(2):
            inner = joined_rows(grad_tile, 0, from_above, from_below, s, c)
            outer = joined_rows(grad_side, 1, from_above, from_below, s, c)
            new_tile[s, c] = inner
            new_side[s, c] = outer
            near[s, c] = jnp.where(pick, inner, outer)
            far[s, c] = jnp.where(pick, outer, inner)


def step_body(
    tile, side_block, grad_tile, grad_side, near, far, new_tile, new_side, to_below, to_above
):
    layers, _, side, _ = tile.shape
    half = side // 2
    pick = halves(side, odd_column())
    col, cols = lax.axis_index("col"), lax.axis_size("col")
    lane = lanes((side, side))
    first = jnp.where(col + 1 < cols, 0, half)
    last = jnp.where(col > 0, side, half)
    on_grid = (lane >= first) & (lane < last)
    for s in range(layers):
        for c in range(2):
            inner = grad_tile[s, c] + jnp.where(pick, near[s, c], far[s, c])
            outer = grad_side[s, c] + jnp.where(pick, far[s, c], near[s, c])
            inner = tile[s, c] - LEARNING_RATE * inner
            outer = jnp.where(on_grid, side_block[s, c] - LEARNING_RATE * outer, 0.0)
            new_tile[s, c] = inner
            new_side[s, c] = outer
            rows_out((inner, outer), s, c, to_below, to_above, half)


def last_rows_body(grad_tile, grad_side, from_above, from_below, new_tile, near, far):
    layers, _, side, _ = grad_tile.shape
    half = side // 2
    pick = halves(side, odd_column())
    for s in range(layers):
        outer = []
        for c in range(2):
            new_tile[s, c] = joined_rows(grad_tile, 0, from_above, from_below, s, c)
            outer.append(joined_rows(grad_side, 1, from_above, from_below, s, c))
        turned = pltpu.roll(outer[1], half, 1)
        near[s] = jnp.where(pick, turned, outer[0])
        far[s] = jnp.where(pick, outer[0], turned)


def last_body(tile, grad_tile, near, far, out, held, sems):
    layers, _, side, _ = tile.shape
    pick = halves(side, odd_column())
    copies = [pltpu.make_async_copy(held.at[s], out.at[s], sems.at[s]) for s in range(layers)]
    for s in range(layers):
        imag = pltpu.roll(jnp.where(pick, far[s], near[s]), side // 2, 1)
        for c, part in enumerate((jnp.where(pick, near[s], far[s]), imag)):
            held[s, c] = tile[s, c] - LEARNING_RATE * (grad_tile[s, c] + part)
        copies[s].start()
    for copy in copies:
        copy.wait()


def call(body, shapes, *operands, specs=None, outs=None, grid=(), scratch=(), name=None, flops=0):
    return pl.pallas_call(
        body,
        out_shape=[jax.ShapeDtypeStruct(shape, F32) for shape in shapes],
        grid=grid,
        in_specs=specs or [VMEM] * len(operands),
        out_specs=outs or [VMEM] * len(shapes),
        scratch_shapes=list(scratch),
        compiler_params=PARAMS,
        name=name,
        cost_estimate=pl.CostEstimate(
            flops=flops,
            bytes_accessed=sum(4 * math.prod(shape) for shape in shapes),
            transcendentals=0,
        ),
    )(*operands)


def across(axis, near, far):
    count = lax.axis_size(axis)
    trades = []
    for block, start in ((near, 1), (far, 0)):
        pairs = [(i, i + 1) for i in range(start, count - 1, 2)]
        trades.append(lax.ppermute(block, axis, pairs + [(j, i) for i, j in pairs]))
    return trades


def shards(object_field, probe, measured, positions, counts):
    layers, _, side, _ = object_field.shape
    half = side // 2
    slots = positions.shape[2]
    places = jnp.concatenate([positions.reshape(2 * slots), counts.reshape(1)])
    tables = jnp.where(counts[0, 0] > 0, jnp.asarray(make_tables(side)), 0)
    whole, packed, strips = (layers, 2, side, side), (layers, side, side), (2, layers, 2, half, side)
    scratch = (
        pltpu.VMEM((layers * 2 * slots, 2 * side, side), F32),
        pltpu.VMEM((layers, 2, slots, side, side), F32),
        pltpu.VMEM((layers - 1, 2, slots, side, side), F32),
    )
    products = 2 * layers
    flops = products * 2 * 3 * 2 * (2 * side) ** 2 * (slots * side)
    tile = object_field
    held = (pltpu.VMEM(whole, F32), pltpu.SemaphoreType.DMA((layers,)))
    layer = pl.BlockSpec((1, side, side), lambda s: (s, 0, 0))
    sent = call(
        pack_body, (packed, packed), tile,
        specs=[pl.BlockSpec((1, 2, side, side), lambda s: (s, 0, 0, 0))], outs=[layer, layer],
        grid=(layers,), name="pack",
    )
    side_block, *sent = call(
        halo_body, (whole, strips, strips), tile, *across("col", *sent), name="halo"
    )
    for iteration in range(ITERS):
        from_above, from_below = across("row", *sent)
        parts, *sent = call(
            slots_body,
            ((layers, 2, slots, side, side), strips, strips),
            places, tile, side_block, from_above, from_below, probe, measured, tables,
            specs=[SMEM] + [VMEM] * 7,
            scratch=scratch,
            name="slots",
            flops=flops,
        )
        grad_tile, grad_side = call(
            keep_body, (whole, whole), places, parts, specs=[SMEM, VMEM], name="keep"
        )
        from_above, from_below = across("row", *sent)
        if iteration + 1 < ITERS:
            grad_tile, grad_side, *sent = call(
                middle_body, (whole, whole, whole, whole), grad_tile, grad_side, from_above, from_below, name="middle"
            )
            tile, side_block, *sent = call(
                step_body,
                (whole, whole, strips, strips),
                tile, side_block, grad_tile, grad_side, *across("col", *sent),
                name="step",
            )
        else:
            grad_tile, *sent = call(
                last_rows_body, (whole, packed, packed), grad_tile, grad_side, from_above, from_below, name="last_rows"
            )
            (tile,) = call(
                last_body, (whole,), tile, grad_tile, *across("col", *sent), outs=[ANY], scratch=held, name="last"
            )
    return tile


def solution(mesh):
    placed = (
        P(None, None, "row", "col"),
        P(),
        P("row", "col", None, None, None),
        P("row", "col", None, None),
        P("row", "col"),
    )
    return jax.shard_map(
        shards, mesh=mesh, in_specs=placed, out_specs=P(None, None, "row", "col"), check_vma=False
    )
```
